32 devices in a mesh: wide: 8 (over z, x), deep: 4 (over y, core).
Axes of the slice: x: 2, y: 2, z: 4, core: 2. Of those that a mesh axis runs over, the one named last changes fastest.
Arguments:
- density: bfloat16 [2048, 64, 128], P(('wide', 'deep')), may hold values from -0.1796875 to 0.1796875
- basis_in: bfloat16 [2048, 64, 128], P(('wide', 'deep')), may hold values from -0.5 to 0.5
- basis_out: bfloat16 [2048, 64, 128], P(('wide', 'deep')), may hold values from -0.75 to 0.75
- points: bfloat16 [2048, 3, 128], P(('wide', 'deep')), may hold values from 0 to 4
- nodes: bfloat16 [2048, 3, 64], P(('wide', 'deep')), may hold values from 0 to 16
- near_rows: int32 [2048, 27], P(('wide', 'deep')), may hold values from 0 to 2047, as said below
- send_leaf: int32 [32, 32, 8], P(('wide', 'deep')), may hold values from 0 to 63
- adm_slot: int32 [2048, 96], P(('wide', 'deep')), may hold values from 0 to 255
Outputs:
- potential: float32 [2048, 64, 128], P(('wide', 'deep'))
The draws below stay inside these ranges and needn't reach their ends.
Inputs may be any that keep to these rules, and one draw needn't show every extreme that they name: near_rows[j, 0] = j. Every other entry names a leaf of the device of leaf j, of the next device along deep, or of the next device along wide; leaf j lies on device j // 64, numbered wide index * 4 + deep index.
All inputs are finite; a program needn't handle non-finite values.
Results may differ from the reference program's by a relative error of at most 0.0033.
Values may be sent and summed in bfloat16 or wider, within the bound.
A program may use at most 128 MiB of HBM per device.

```python
import jax
import jax.numpy as jnp
from jax import lax

LEAF = 128
RANK = 64
NRHS = 64
NEAR = 27
ADM = 96
LEAF_DEV = 64
NEED = 256
NLEAF = 2048
CAP = 8
N_WIDE = 8
N_DEEP = 4
DEVICES = 32


def draw_near_rows(key, part):
    key = jax.random.fold_in(key, 11)
    total = LEAF_DEV * N_WIDE * N_DEEP
    leaf_ids = jnp.arange(total, dtype=jnp.int32)
    owner_dev = leaf_ids // LEAF_DEV
    wide_pos = owner_dev // N_DEEP
    deep_pos = owner_dev % N_DEEP
    key_region, key_chosen = jax.random.split(key)
    region = jax.random.randint(key_region, (total, NEAR - 1), 0, 3)
    region = jnp.where((region == 1) & (deep_pos[:, None] == N_DEEP - 1), 0, region)
    region = jnp.where((region == 2) & (wide_pos[:, None] == N_WIDE - 1), 0, region)
    target_dev = owner_dev[:, None] + jnp.where(region == 1, 1, 0) + jnp.where(region == 2, N_DEEP, 0)
    chosen = jax.random.randint(key_chosen, (total, NEAR - 1), 0, LEAF_DEV)
    others = target_dev * LEAF_DEV + chosen
    return jnp.concatenate([leaf_ids[:, None], others], axis=1).astype(jnp.int32)


def touch_ends(result, own_key, smallest, largest):
    spot = [jax.random.randint(jax.random.fold_in(own_key, axis), (), 0, length) for axis, length in enumerate(result.shape)]
    main_axis = result.shape.index(max(result.shape))
    neighbour = spot[:main_axis] + [(spot[main_axis] + 1) % result.shape[main_axis]] + spot[main_axis + 1:]
    return result.at[tuple(spot)].set(smallest).at[tuple(neighbour)].set(largest)


def shard_levels(own_key, shape, cuts, least, high):
    level, own = 1.0, jax.random.fold_in(own_key, 6)
    for axis_at, parts in cuts:
        draws = jnp.exp(jax.random.uniform(jax.random.fold_in(own, axis_at), (parts,), jnp.float32, least / len(cuts), high / len(cuts)))
        level = level * jnp.repeat(draws, shape[axis_at] // parts).reshape([-1 if axis == axis_at else 1 for axis in range(len(shape))])
    return level


def bell_draw(own_key, shape, width, limit, cuts=(), held_as=jnp.bfloat16):
    values = jax.random.normal(own_key, shape, jnp.float32) * width
    if len(cuts) > 0:
        values = shard_levels(own_key, shape, cuts, -0.22, 0.18) * values
    return jnp.clip(values, min=-limit, max=limit).astype(held_as)


def setup_inputs(seed: int = 0) -> dict:
    keys = jax.random.split(jax.random.key(seed), 9)
    density = bell_draw(keys[0], (NLEAF, NRHS, LEAF), 0.03, 0.1796875, ((0, 32),))
    basis_in = bell_draw(keys[1], (NLEAF, RANK, LEAF), LEAF ** -0.5, 0.5, ((0, 32),))
    basis_out = bell_draw(keys[2], (NLEAF, RANK, LEAF), RANK ** -0.5, 0.75, ((0, 32),))
    points = jnp.clip(4.0 * jax.random.uniform(keys[3], (NLEAF, 3, LEAF), jnp.float32) ** shard_levels(keys[3], (NLEAF, 3, LEAF), ((0, 32),), -0.2, 0.2), 0.0, 4.0).astype(jnp.bfloat16)
    nodes = jnp.clip(16.0 * jax.random.uniform(keys[4], (NLEAF, 3, RANK), jnp.float32) ** shard_levels(keys[4], (NLEAF, 3, RANK), ((0, 32),), -0.2, 0.2), 0.0, 16.0).astype(jnp.bfloat16)
    near_rows = draw_near_rows(jax.random.fold_in(keys[8], 71), 0)
    send_leaf = touch_ends(jax.random.randint(keys[6], (DEVICES, DEVICES, CAP), 0, LEAF_DEV), jax.random.fold_in(keys[6], 1), 0, LEAF_DEV - 1).astype(jnp.int32)
    adm_slot = touch_ends(jax.random.randint(keys[7], (NLEAF, ADM), 0, NEED), jax.random.fold_in(keys[7], 1), 0, NEED - 1).astype(jnp.int32)
    return {"density": density, "basis_in": basis_in, "basis_out": basis_out, "points": points, "nodes": nodes, "near_rows": near_rows, "send_leaf": send_leaf, "adm_slot": adm_slot}


SOFTENING = 0.25

def pair_kernel(targets, sources):
    differ = targets[..., 0, :, None] - sources[..., 0, None, :]
    squared = differ * differ
    for coord in range(1, 3):
        differ = targets[..., coord, :, None] - sources[..., coord, None, :]
        squared = squared + differ * differ
    return 1.0 / jnp.sqrt(squared + SOFTENING)

def reference(density, basis_in, basis_out, points, nodes, near_rows, send_leaf, adm_slot):
    total = density.shape[0]
    coefficients = jnp.einsum('jrp,jnp->jrn', basis_in.astype(jnp.float32), density.astype(jnp.float32)).astype(jnp.bfloat16)
    coefficients = lax.optimization_barrier(coefficients)
    row_ids = jnp.arange(total, dtype=jnp.int32)
    source_dev = (adm_slot // CAP).astype(jnp.int32)
    within = (adm_slot % CAP).astype(jnp.int32)
    column = source_dev * LEAF_DEV + send_leaf[source_dev, (row_ids // LEAF_DEV)[:, None], within]
    blocks = total // LEAF_DEV

    def far_block(items):
        columns, row_nodes, out_basis = items
        gathered = coefficients[columns].astype(jnp.float32)
        far_nodes = nodes[columns].astype(jnp.float32)
        coupling = pair_kernel(row_nodes[:, None].astype(jnp.float32), far_nodes).astype(jnp.bfloat16)
        coupling = lax.optimization_barrier(coupling).astype(jnp.float32)
        far_coef = jnp.einsum('iarb,iabn->irn', coupling, gathered).astype(jnp.bfloat16)
        far_coef = lax.optimization_barrier(far_coef).astype(jnp.float32)
        return jnp.einsum('irn,irp->inp', far_coef, out_basis.astype(jnp.float32))
    far_field = lax.map(far_block, (column.reshape(blocks, LEAF_DEV, ADM), nodes.reshape(blocks, LEAF_DEV, 3, RANK), basis_out.reshape(blocks, LEAF_DEV, RANK, LEAF)))
    far_field = far_field.reshape(total, NRHS, LEAF)

    def near_step(totals, items):
        dens_block, own_points, targets = items
        target_points = points[targets].astype(jnp.float32)
        kernel_block = pair_kernel(target_points, own_points[:, None].astype(jnp.float32)).astype(jnp.bfloat16)
        kernel_block = lax.optimization_barrier(kernel_block).astype(jnp.float32)
        partial_sums = jnp.einsum('jkab,jnb->jkna', kernel_block, dens_block.astype(jnp.float32))
        totals = totals.at[targets.reshape(-1)].add(partial_sums.reshape(-1, NRHS, LEAF))
        return (totals, None)
    start_totals = jnp.zeros((total, NRHS, LEAF), jnp.float32)
    near_field, _ = lax.scan(near_step, start_totals, (density.reshape(blocks, LEAF_DEV, NRHS, LEAF), points.reshape(blocks, LEAF_DEV, 3, LEAF), near_rows.reshape(blocks, LEAF_DEV, NEAR)))
    return far_field + near_field
```

```python
import jax
import jax.numpy as jnp
from jax import lax
from jax.experimental import pallas as pl
from jax.experimental.pallas import tpu as pltpu
from jax.sharding import PartitionSpec as P

SOFTENING = 0.25
DEPTH = 16
GROUP = 8
VMEM_BYTES = 48 * 1024 * 1024
HALF_MATH = False


def passed_along(x, axis, by):
    length = lax.axis_size(axis)
    pairs = [(i, i + by) for i in range(length) if 0 <= i + by < length]
    return lax.ppermute(x, axis, pairs)


def whole(space=pltpu.VMEM):
    return pl.BlockSpec(memory_space=space)


def params():
    return pltpu.CompilerParams(vmem_limit_bytes=VMEM_BYTES)


def split_three(x):
    high = lax.reduce_precision(x, 8, 7)
    rest = x - high
    middle = lax.reduce_precision(rest, 8, 7)
    return [high, middle, rest - middle]


def as_targets(coords):
    x = coords.astype(jnp.float32)
    square = jnp.sum(x * x, axis=1, keepdims=True)
    ones = jnp.ones_like(square)
    rows = [x] + split_three(square) + [ones] * 3 + [jnp.zeros_like(square)] * (DEPTH - 9)
    return jnp.concatenate(rows, axis=1).astype(jnp.bfloat16)


def as_sources(coords):
    x = coords.astype(jnp.float32)
    square = jnp.sum(x * x, axis=1, keepdims=True) + SOFTENING
    ones = jnp.ones_like(square)
    rows = [-2.0 * x] + [ones] * 3 + split_three(square) + [jnp.zeros_like(square)] * (DEPTH - 9)
    return jnp.concatenate(rows, axis=1).astype(jnp.bfloat16)


def inverse_root(squared):
    if HALF_MATH:
        return lax.rsqrt(squared.astype(jnp.bfloat16))
    return lax.rsqrt(squared).astype(jnp.bfloat16)


def turned(block):
    return jnp.transpose(block.astype(jnp.float32)).astype(jnp.bfloat16)


def outgoing_kernel(send_ref, basis_ref, density_ref, out_ref, coef_ref):
    leaves, rank, _ = basis_ref.shape
    half = rank // 2

    def make(j, carry):
        coef = lax.dot_general(
            basis_ref[j], density_ref[j], (((1,), (1,)), ((), ())),
            preferred_element_type=jnp.float32,
        )
        coef_ref[j] = jnp.concatenate([coef[:half], coef[half:]], axis=1).astype(jnp.bfloat16)
        return carry

    lax.fori_loop(0, leaves, make, 0, unroll=4)

    def pick(q, carry):
        out_ref[q] = coef_ref[send_ref[q]]
        return carry

    lax.fori_loop(0, out_ref.shape[0], pick, 0, unroll=8)


def outgoing_blocks(send, basis_in, density):
    leaves, rank, _ = basis_in.shape
    fields = density.shape[1]
    shape = (rank // 2, 2 * fields)
    return pl.pallas_call(
        outgoing_kernel,
        out_shape=jax.ShapeDtypeStruct((send.shape[0],) + shape, jnp.bfloat16),
        in_specs=[whole(pltpu.SMEM), whole(), whole()],
        out_specs=whole(),
        scratch_shapes=[pltpu.VMEM((leaves,) + shape, jnp.bfloat16)],
        compiler_params=params(),
        name="outgoing",
    )(send, basis_in, density)


def near_kernel(codes_ref, sources_ref, targets_ref, density_ref, own_ref, deep_ref, wide_ref, acc_ref):
    leaves = sources_ref.shape[0]
    near = codes_ref.shape[1]
    width = sources_ref.shape[2]
    acc_ref[...] = jnp.zeros_like(acc_ref)

    def column(j, carry):
        source = turned(sources_ref[j])
        fields = density_ref[j]
        saved = []
        for first in range(0, near, 2):
            picks = [codes_ref[j, k] for k in range(first, min(first + 2, near))]
            tiles = [targets_ref[t] for t in picks]
            tile = tiles[0] if len(tiles) == 1 else jnp.concatenate(tiles, axis=1)
            squared = jnp.dot(source, tile, preferred_element_type=jnp.float32)
            block = inverse_root(squared)
            saved.append((picks, block))
        parts = [(p, jnp.dot(fields, b, preferred_element_type=jnp.float32)) for p, b in saved]
        for picks, part in parts:
            for place, t in enumerate(picks):
                acc_ref[t] += part[:, place * width:(place + 1) * width]
        return carry

    lax.fori_loop(0, leaves, column, 0)
    own_ref[...] = acc_ref[:leaves]
    deep_ref[...] = acc_ref[leaves:2 * leaves].astype(jnp.bfloat16)
    wide_ref[...] = acc_ref[2 * leaves:].astype(jnp.bfloat16)


def near_sums(codes, sources, targets, density):
    leaves, fields, width = density.shape
    pairs = leaves * codes.shape[1] * width * width
    return pl.pallas_call(
        near_kernel,
        out_shape=[
            jax.ShapeDtypeStruct(density.shape, jnp.float32),
            jax.ShapeDtypeStruct(density.shape, jnp.bfloat16),
            jax.ShapeDtypeStruct(density.shape, jnp.bfloat16),
        ],
        in_specs=[whole(pltpu.SMEM), whole(), whole(), whole()],
        out_specs=[whole(), whole(), whole()],
        scratch_shapes=[pltpu.VMEM((3 * leaves, fields, width), jnp.float32)],
        compiler_params=params(),
        cost_estimate=pl.CostEstimate(
            flops=pairs * 600, bytes_accessed=16 * 2**20, transcendentals=pairs
        ),
        name="near",
    )(codes, sources, targets, density)


def far_kernel(slots_ref, nodes_ref, far_nodes_ref, table_ref, basis_ref, out_ref):
    leaves, _, rank = nodes_ref.shape
    count = slots_ref.shape[1]
    half = rank // 2
    fields = table_ref.shape[2] // 2
    lanes = lax.broadcasted_iota(jnp.int32, (DEPTH, 4 * half), 1)

    def four(side, picks):
        tile = far_nodes_ref[picks[3], side]
        for place in (2, 1, 0):
            tile = jnp.where(lanes < (place + 1) * half, far_nodes_ref[picks[place], side], tile)
        return tile

    def row(i, carry):
        own = turned(nodes_ref[i])
        saved = []
        for first in range(0, count, GROUP):
            picks = [slots_ref[i, a] for a in range(first, first + GROUP)]
            coupling = []
            for side in range(2):
                tile = jnp.concatenate([four(side, picks[:4]), four(side, picks[4:])], axis=1)
                squared = jnp.dot(own, tile, preferred_element_type=jnp.float32)
                coupling.append(inverse_root(squared))
            saved.append((picks, jnp.concatenate(coupling, axis=0)))
        columns = jnp.concatenate([table_ref[s] for picks, _ in saved for s in picks], axis=0)
        total = jnp.dot(jnp.concatenate([b for _, b in saved], axis=1), columns, preferred_element_type=jnp.float32)
        far_coef = total[:rank, :fields] + total[rank:, fields:]
        out_ref[i] = jnp.dot(
            turned(far_coef), basis_ref[i], preferred_element_type=jnp.float32
        )
        return carry

    lax.fori_loop(0, leaves, row, 0, unroll=2)


def far_sums(slots, nodes, far_nodes, table, basis_out):
    leaves, rank, width = basis_out.shape
    fields = table.shape[2] // 2
    pairs = leaves * slots.shape[1] * rank * rank
    return pl.pallas_call(
        far_kernel,
        out_shape=jax.ShapeDtypeStruct((leaves, fields, width), jnp.float32),
        in_specs=[whole(pltpu.SMEM)] + [whole()] * 4,
        out_specs=whole(),
        compiler_params=params(),
        cost_estimate=pl.CostEstimate(
            flops=pairs * 600, bytes_accessed=8 * 2**20, transcendentals=pairs
        ),
        name="far",
    )(slots, nodes, far_nodes, table, basis_out)


def halves_repeated(far_nodes):
    half = far_nodes.shape[2] // 2
    sides = [jnp.concatenate([far_nodes[:, :, s * half:(s + 1) * half]] * 4, axis=2) for s in range(2)]
    return jnp.stack(sides, axis=1)


def shards(density, basis_in, basis_out, points, nodes, near_rows, send_leaf, adm_slot):
    leaves, fields, leaf_size = density.shape
    rank_size = basis_in.shape[1]
    deep_count = lax.axis_size("deep")
    devices = lax.axis_size("wide") * deep_count
    capacity = send_leaf.shape[2]
    axes = ("wide", "deep")
    send = send_leaf.reshape(devices * capacity)
    deep_points = passed_along(points, "deep", -1)
    wide_points = passed_along(points, "wide", -1)
    outgoing = outgoing_blocks(send, basis_in, density)
    outgoing = outgoing.reshape(devices, capacity * outgoing.shape[1], outgoing.shape[2])
    out_nodes = nodes.reshape(leaves, -1)[send].reshape(devices, capacity, 3 * rank_size)
    table_nodes = lax.all_to_all(out_nodes, axes, split_axis=0, concat_axis=0, tiled=True)
    table = lax.all_to_all(outgoing, axes, split_axis=0, concat_axis=0, tiled=True)
    table = table.reshape(devices * capacity, rank_size // 2, 2 * fields)
    far_nodes = as_targets(table_nodes.reshape(devices * capacity, 3, rank_size))
    far_nodes = halves_repeated(far_nodes)

    my_device = lax.axis_index("wide") * deep_count + lax.axis_index("deep")
    point_table = as_targets(jnp.concatenate([points, deep_points, wide_points], axis=0))
    offset = near_rows // leaves - my_device
    region = jnp.where(offset == 0, 0, jnp.where(offset == 1, 1, 2))
    codes = region * leaves + near_rows % leaves
    own, for_deep, for_wide = near_sums(codes, as_sources(points), point_table, density)
    from_deep = passed_along(for_deep, "deep", 1)
    from_wide = passed_along(for_wide, "wide", 1)
    far_field = far_sums(adm_slot, as_sources(nodes), far_nodes, table, basis_out)
    return far_field + (own + from_deep.astype(jnp.float32) + from_wide.astype(jnp.float32))


def solution(mesh):
    split = ("wide", "deep")
    in_specs = (
        P(split, None, None),
        P(split, None, None),
        P(split, None, None),
        P(split, None, None),
        P(split, None, None),
        P(split, None),
        P(split, None, None),
        P(split, None),
    )
    return jax.shard_map(
        shards, mesh=mesh, in_specs=in_specs, out_specs=P(split, None, None), check_vma=False
    )
```

```python
import jax
import jax.numpy as jnp
from jax import lax
from jax.experimental import pallas as pl
from jax.experimental.pallas import tpu as pltpu
from jax.sharding import PartitionSpec as P

SOFTENING = 0.25
DEPTH = 16
GROUP = 8
VMEM_BYTES = 48 * 1024 * 1024
HALF_MATH = False
NEAR_TOGETHER = 4
NEAR_LAG = 10
FAR_TOGETHER = 4
FAR_LAG = 10


def passed_along(x, axis, by):
    length = lax.axis_size(axis)
    pairs = [(i, i + by) for i in range(length) if 0 <= i + by < length]
    return lax.ppermute(x, axis, pairs)


def whole(space=pltpu.VMEM):
    return pl.BlockSpec(memory_space=space)


def params():
    return pltpu.CompilerParams(vmem_limit_bytes=VMEM_BYTES)


def split_three(x):
    high = lax.reduce_precision(x, 8, 7)
    rest = x - high
    middle = lax.reduce_precision(rest, 8, 7)
    return [high, middle, rest - middle]


def as_targets(coords):
    x = coords.astype(jnp.float32)
    square = jnp.sum(x * x, axis=1, keepdims=True)
    ones = jnp.ones_like(square)
    rows = [x] + split_three(square) + [ones] * 3 + [jnp.zeros_like(square)] * (DEPTH - 9)
    return jnp.concatenate(rows, axis=1).astype(jnp.bfloat16)


def as_sources(coords):
    x = coords.astype(jnp.float32)
    square = jnp.sum(x * x, axis=1, keepdims=True) + SOFTENING
    ones = jnp.ones_like(square)
    rows = [-2.0 * x] + [ones] * 3 + split_three(square) + [jnp.zeros_like(square)] * (DEPTH - 9)
    return jnp.concatenate(rows, axis=1).astype(jnp.bfloat16)


def inverse_root(squared):
    if HALF_MATH:
        return lax.rsqrt(squared.astype(jnp.bfloat16))
    return lax.rsqrt(squared).astype(jnp.bfloat16)


def turned(block):
    return jnp.transpose(block.astype(jnp.float32)).astype(jnp.bfloat16)


def outgoing_kernel(send_ref, basis_ref, density_ref, out_ref, coef_ref):
    leaves, rank, _ = basis_ref.shape
    half = rank // 2

    def make(j, carry):
        coef = lax.dot_general(
            basis_ref[j], density_ref[j], (((1,), (1,)), ((), ())),
            preferred_element_type=jnp.float32,
        )
        coef_ref[j] = jnp.concatenate([coef[:half], coef[half:]], axis=1).astype(jnp.bfloat16)
        return carry

    lax.fori_loop(0, leaves, make, 0, unroll=4)

    def pick(q, carry):
        out_ref[q] = coef_ref[send_ref[q]]
        return carry

    lax.fori_loop(0, out_ref.shape[0], pick, 0, unroll=8)


def outgoing_blocks(send, basis_in, density):
    leaves, rank, _ = basis_in.shape
    fields = density.shape[1]
    shape = (rank // 2, 2 * fields)
    return pl.pallas_call(
        outgoing_kernel,
        out_shape=jax.ShapeDtypeStruct((send.shape[0],) + shape, jnp.bfloat16),
        in_specs=[whole(pltpu.SMEM), whole(), whole()],
        out_specs=whole(),
        scratch_shapes=[pltpu.VMEM((leaves,) + shape, jnp.bfloat16)],
        compiler_params=params(),
        name="outgoing",
    )(send, basis_in, density)


def near_kernel(codes_ref, sources_ref, targets_ref, density_ref, own_ref, deep_ref, wide_ref, acc_ref):
    leaves = sources_ref.shape[0]
    near = codes_ref.shape[1]
    width = sources_ref.shape[2]
    acc_ref[...] = jnp.zeros_like(acc_ref)

    def columns(step, carry):
        first_leaf = step * NEAR_TOGETHER
        waiting = []

        def apply(leaf, picks, block):
            part = jnp.dot(density_ref[leaf], block, preferred_element_type=jnp.float32)
            for place, t in enumerate(picks):
                acc_ref[t] += part[:, place * width:(place + 1) * width]

        for ahead in range(NEAR_TOGETHER):
            j = first_leaf + ahead
            source = turned(sources_ref[j])
            for first in range(0, near, 2):
                picks = [codes_ref[j, k] for k in range(first, min(first + 2, near))]
                tiles = [targets_ref[t] for t in picks]
                tile = tiles[0] if len(tiles) == 1 else jnp.concatenate(tiles, axis=1)
                squared = jnp.dot(source, tile, preferred_element_type=jnp.float32)
                waiting.append((j, picks, inverse_root(squared)))
                if len(waiting) > NEAR_LAG:
                    apply(*waiting.pop(0))
        for item in waiting:
            apply(*item)
        return carry

    lax.fori_loop(0, leaves // NEAR_TOGETHER, columns, 0)
    own_ref[...] = acc_ref[:leaves]
    deep_ref[...] = acc_ref[leaves:2 * leaves].astype(jnp.bfloat16)
    wide_ref[...] = acc_ref[2 * leaves:].astype(jnp.bfloat16)


def near_sums(codes, sources, targets, density):
    leaves, fields, width = density.shape
    pairs = leaves * codes.shape[1] * width * width
    return pl.pallas_call(
        near_kernel,
        out_shape=[
            jax.ShapeDtypeStruct(density.shape, jnp.float32),
            jax.ShapeDtypeStruct(density.shape, jnp.bfloat16),
            jax.ShapeDtypeStruct(density.shape, jnp.bfloat16),
        ],
        in_specs=[whole(pltpu.SMEM), whole(), whole(), whole()],
        out_specs=[whole(), whole(), whole()],
        scratch_shapes=[pltpu.VMEM((3 * leaves, fields, width), jnp.float32)],
        compiler_params=params(),
        cost_estimate=pl.CostEstimate(
            flops=pairs * 600, bytes_accessed=16 * 2**20, transcendentals=pairs
        ),
        name="near",
    )(codes, sources, targets, density)


def far_kernel(slots_ref, nodes_ref, far_nodes_ref, table_ref, basis_ref, out_ref):
    leaves, _, rank = nodes_ref.shape
    count = slots_ref.shape[1]
    half = rank // 2
    fields = table_ref.shape[2] // 2
    lanes = lax.broadcasted_iota(jnp.int32, (DEPTH, 4 * half), 1)

    def four(side, picks):
        tile = far_nodes_ref[picks[3], side]
        for place in (2, 1, 0):
            tile = jnp.where(lanes < (place + 1) * half, far_nodes_ref[picks[place], side], tile)
        return tile

    def rows(step, carry):
        first_leaf = step * FAR_TOGETHER
        waiting = []
        totals = {}

        def apply(ahead, picks, block):
            columns = jnp.concatenate([table_ref[s] for s in picks], axis=0)
            part = jnp.dot(block, columns, preferred_element_type=jnp.float32)
            totals[ahead] = totals[ahead] + part if ahead in totals else part

        def finish(ahead):
            total = totals[ahead]
            far_coef = total[:rank, :fields] + total[rank:, fields:]
            i = first_leaf + ahead
            out_ref[i] = jnp.dot(turned(far_coef), basis_ref[i], preferred_element_type=jnp.float32)

        for ahead in range(FAR_TOGETHER):
            i = first_leaf + ahead
            own = turned(nodes_ref[i])
            for first in range(0, count, GROUP):
                picks = [slots_ref[i, a] for a in range(first, first + GROUP)]
                coupling = []
                for side in range(2):
                    tile = jnp.concatenate([four(side, picks[:4]), four(side, picks[4:])], axis=1)
                    squared = jnp.dot(own, tile, preferred_element_type=jnp.float32)
                    coupling.append(inverse_root(squared))
                waiting.append((ahead, picks, jnp.concatenate(coupling, axis=0)))
                if len(waiting) > FAR_LAG:
                    apply(*waiting.pop(0))
        for item in waiting:
            apply(*item)
        for ahead in range(FAR_TOGETHER):
            finish(ahead)
        return carry

    lax.fori_loop(0, leaves // FAR_TOGETHER, rows, 0)


def far_sums(slots, nodes, far_nodes, table, basis_out):
    leaves, rank, width = basis_out.shape
    fields = table.shape[2] // 2
    pairs = leaves * slots.shape[1] * rank * rank
    return pl.pallas_call(
        far_kernel,
        out_shape=jax.ShapeDtypeStruct((leaves, fields, width), jnp.float32),
        in_specs=[whole(pltpu.SMEM)] + [whole()] * 4,
        out_specs=whole(),
        compiler_params=params(),
        cost_estimate=pl.CostEstimate(
            flops=pairs * 600, bytes_accessed=8 * 2**20, transcendentals=pairs
        ),
        name="far",
    )(slots, nodes, far_nodes, table, basis_out)


def halves_repeated(far_nodes):
    half = far_nodes.shape[2] // 2
    sides = [jnp.concatenate([far_nodes[:, :, s * half:(s + 1) * half]] * 4, axis=2) for s in range(2)]
    return jnp.stack(sides, axis=1)


def shards(density, basis_in, basis_out, points, nodes, near_rows, send_leaf, adm_slot):
    leaves, fields, leaf_size = density.shape
    rank_size = basis_in.shape[1]
    deep_count = lax.axis_size("deep")
    devices = lax.axis_size("wide") * deep_count
    capacity = send_leaf.shape[2]
    axes = ("wide", "deep")
    send = send_leaf.reshape(devices * capacity)
    deep_points = passed_along(points, "deep", -1)
    wide_points = passed_along(points, "wide", -1)
    outgoing = outgoing_blocks(send, basis_in, density)
    outgoing = outgoing.reshape(devices, capacity * outgoing.shape[1], outgoing.shape[2])
    out_nodes = nodes.reshape(leaves, -1)[send].reshape(devices, capacity, 3 * rank_size)
    table_nodes = lax.all_to_all(out_nodes, axes, split_axis=0, concat_axis=0, tiled=True)
    table = lax.all_to_all(outgoing, axes, split_axis=0, concat_axis=0, tiled=True)
    table = table.reshape(devices * capacity, rank_size // 2, 2 * fields)
    far_nodes = as_targets(table_nodes.reshape(devices * capacity, 3, rank_size))
    far_nodes = halves_repeated(far_nodes)

    my_device = lax.axis_index("wide") * deep_count + lax.axis_index("deep")
    point_table = as_targets(jnp.concatenate([points, deep_points, wide_points], axis=0))
    offset = near_rows // leaves - my_device
    region = jnp.where(offset == 0, 0, jnp.where(offset == 1, 1, 2))
    codes = region * leaves + near_rows % leaves
    own, for_deep, for_wide = near_sums(codes, as_sources(points), point_table, density)
    from_deep = passed_along(for_deep, "deep", 1)
    from_wide = passed_along(for_wide, "wide", 1)
    far_field = far_sums(adm_slot, as_sources(nodes), far_nodes, table, basis_out)
    return far_field + (own + from_deep.astype(jnp.float32) + from_wide.astype(jnp.float32))


def solution(mesh):
    split = ("wide", "deep")
    in_specs = (
        P(split, None, None),
        P(split, None, None),
        P(split, None, None),
        P(split, None, None),
        P(split, None, None),
        P(split, None),
        P(split, None, None),
        P(split, None),
    )
    return jax.shard_map(
        shards, mesh=mesh, in_specs=in_specs, out_specs=P(split, None, None), check_vma=False
    )
```

```python
import jax
import jax.numpy as jnp
from jax import lax
from jax.experimental import pallas as pl
from jax.experimental.pallas import tpu as pltpu
from jax.sharding import PartitionSpec as P

SOFTENING = 0.25
DEPTH = 16
GROUP = 8
VMEM_BYTES = 48 * 1024 * 1024
HALF_MATH = False
NEAR_TOGETHER = 4
NEAR_LAG = 10
FAR_TOGETHER = 4
FAR_LAG = 10


def passed_along(x, axis, by):
    length = lax.axis_size(axis)
    pairs = [(i, i + by) for i in range(length) if 0 <= i + by < length]
    return lax.ppermute(x, axis, pairs)


def whole(space=pltpu.VMEM):
    return pl.BlockSpec(memory_space=space)


def params():
    return pltpu.CompilerParams(vmem_limit_bytes=VMEM_BYTES)


def split_three(x):
    high = lax.reduce_precision(x, 8, 7)
    rest = x - high
    middle = lax.reduce_precision(rest, 8, 7)
    return [high, middle, rest - middle]


def as_targets(coords):
    x = coords.astype(jnp.float32)
    square = jnp.sum(x * x, axis=1, keepdims=True)
    ones = jnp.ones_like(square)
    rows = [x] + split_three(square) + [ones] * 3 + [jnp.zeros_like(square)] * (DEPTH - 9)
    return jnp.concatenate(rows, axis=1).astype(jnp.bfloat16)


def as_sources(coords):
    x = coords.astype(jnp.float32)
    square = jnp.sum(x * x, axis=1, keepdims=True) + SOFTENING
    ones = jnp.ones_like(square)
    rows = [-2.0 * x] + [ones] * 3 + split_three(square) + [jnp.zeros_like(square)] * (DEPTH - 9)
    return jnp.concatenate(rows, axis=1).astype(jnp.bfloat16)


def inverse_root(squared):
    if HALF_MATH:
        return lax.rsqrt(squared.astype(jnp.bfloat16))
    return lax.rsqrt(squared).astype(jnp.bfloat16)


def turned(block):
    return jnp.transpose(block.astype(jnp.float32)).astype(jnp.bfloat16)


def outgoing_kernel(send_ref, basis_ref, density_ref, out_ref, coef_ref):
    leaves, rank, _ = basis_ref.shape
    half = rank // 2

    def make(j, carry):
        coef = lax.dot_general(
            basis_ref[j], density_ref[j], (((1,), (1,)), ((), ())),
            preferred_element_type=jnp.float32,
        )
        coef_ref[j] = jnp.concatenate([coef[:half], coef[half:]], axis=1).astype(jnp.bfloat16)
        return carry

    lax.fori_loop(0, leaves, make, 0, unroll=4)

    def pick(q, carry):
        out_ref[q] = coef_ref[send_ref[q]]
        return carry

    lax.fori_loop(0, out_ref.shape[0], pick, 0, unroll=8)


def outgoing_blocks(send, basis_in, density):
    leaves, rank, _ = basis_in.shape
    fields = density.shape[1]
    shape = (rank // 2, 2 * fields)
    return pl.pallas_call(
        outgoing_kernel,
        out_shape=jax.ShapeDtypeStruct((send.shape[0],) + shape, jnp.bfloat16),
        in_specs=[whole(pltpu.SMEM), whole(), whole()],
        out_specs=whole(),
        scratch_shapes=[pltpu.VMEM((leaves,) + shape, jnp.bfloat16)],
        compiler_params=params(),
        name="outgoing",
    )(send, basis_in, density)


def near_kernel(codes_ref, sources_ref, targets_ref, density_ref, own_ref, deep_ref, wide_ref, acc_ref):
    leaves = sources_ref.shape[0]
    near = codes_ref.shape[1]
    width = sources_ref.shape[2]
    acc_ref[...] = jnp.zeros_like(acc_ref)

    def columns(step, carry):
        first_leaf = step * NEAR_TOGETHER
        waiting = []

        def apply(leaf, picks, block):
            part = jnp.dot(density_ref[leaf], block, preferred_element_type=jnp.float32)
            for place, t in enumerate(picks):
                acc_ref[t] += part[:, place * width:(place + 1) * width]

        for ahead in range(NEAR_TOGETHER):
            j = first_leaf + ahead
            source = turned(sources_ref[j])
            for first in range(0, near, 2):
                picks = [codes_ref[j, k] for k in range(first, min(first + 2, near))]
                tiles = [targets_ref[t] for t in picks]
                tile = tiles[0] if len(tiles) == 1 else jnp.concatenate(tiles, axis=1)
                squared = jnp.dot(source, tile, preferred_element_type=jnp.float32)
                waiting.append((j, picks, inverse_root(squared)))
                if len(waiting) > NEAR_LAG:
                    apply(*waiting.pop(0))
        for item in waiting:
            apply(*item)
        return carry

    lax.fori_loop(0, leaves // NEAR_TOGETHER, columns, 0)
    own_ref[...] = acc_ref[:leaves]
    deep_ref[...] = acc_ref[leaves:2 * leaves].astype(jnp.bfloat16)
    wide_ref[...] = acc_ref[2 * leaves:].astype(jnp.bfloat16)


def near_sums(codes, sources, targets, density):
    leaves, fields, width = density.shape
    pairs = leaves * codes.shape[1] * width * width
    return pl.pallas_call(
        near_kernel,
        out_shape=[
            jax.ShapeDtypeStruct(density.shape, jnp.float32),
            jax.ShapeDtypeStruct(density.shape, jnp.bfloat16),
            jax.ShapeDtypeStruct(density.shape, jnp.bfloat16),
        ],
        in_specs=[whole(pltpu.SMEM), whole(), whole(), whole()],
        out_specs=[whole(), whole(), whole()],
        scratch_shapes=[pltpu.VMEM((3 * leaves, fields, width), jnp.float32)],
        compiler_params=params(),
        cost_estimate=pl.CostEstimate(
            flops=pairs * 600, bytes_accessed=16 * 2**20, transcendentals=pairs
        ),
        name="near",
    )(codes, sources, targets, density)


def far_kernel(slots_ref, nodes_ref, far_nodes_ref, table_ref, basis_ref, out_ref):
    leaves, _, rank = nodes_ref.shape
    count = slots_ref.shape[1]
    half = rank // 2
    fields = table_ref.shape[2] // 2
    lanes = lax.broadcasted_iota(jnp.int32, (DEPTH, 4 * half), 1)

    def four(side, picks):
        tile = far_nodes_ref[picks[3], side]
        for place in (2, 1, 0):
            tile = jnp.where(lanes < (place + 1) * half, far_nodes_ref[picks[place], side], tile)
        return tile

    def rows(step, carry):
        first_leaf = step * FAR_TOGETHER
        waiting = []
        totals = {}

        def apply(ahead, picks, block):
            columns = jnp.concatenate([table_ref[s] for s in picks], axis=0)
            part = jnp.dot(block, columns, preferred_element_type=jnp.float32)
            totals[ahead] = totals[ahead] + part if ahead in totals else part

        def finish(ahead):
            total = totals[ahead]
            far_coef = total[:rank, :fields] + total[rank:, fields:]
            i = first_leaf + ahead
            out_ref[i] = jnp.dot(turned(far_coef), basis_ref[i], preferred_element_type=jnp.float32)

        for ahead in range(FAR_TOGETHER):
            i = first_leaf + ahead
            own = turned(nodes_ref[i])
            for first in range(0, count, GROUP):
                picks = [slots_ref[i, a] for a in range(first, first + GROUP)]
                coupling = []
                for side in range(2):
                    tile = jnp.concatenate([four(side, picks[:4]), four(side, picks[4:])], axis=1)
                    squared = jnp.dot(own, tile, preferred_element_type=jnp.float32)
                    coupling.append(inverse_root(squared))
                waiting.append((ahead, picks, jnp.concatenate(coupling, axis=0)))
                if len(waiting) > FAR_LAG:
                    apply(*waiting.pop(0))
        for item in waiting:
            apply(*item)
        for ahead in range(FAR_TOGETHER):
            finish(ahead)
        return carry

    lax.fori_loop(0, leaves // FAR_TOGETHER, rows, 0)


def far_sums(slots, nodes, far_nodes, table, basis_out):
    leaves, rank, width = basis_out.shape
    fields = table.shape[2] // 2
    pairs = leaves * slots.shape[1] * rank * rank
    return pl.pallas_call(
        far_kernel,
        out_shape=jax.ShapeDtypeStruct((leaves, fields, width), jnp.float32),
        in_specs=[whole(pltpu.SMEM)] + [whole()] * 4,
        out_specs=whole(),
        compiler_params=params(),
        cost_estimate=pl.CostEstimate(
            flops=pairs * 600, bytes_accessed=8 * 2**20, transcendentals=pairs
        ),
        name="far",
    )(slots, nodes, far_nodes, table, basis_out)


def halves_repeated(far_nodes):
    half = far_nodes.shape[2] // 2
    sides = [jnp.concatenate([far_nodes[:, :, s * half:(s + 1) * half]] * 4, axis=2) for s in range(2)]
    return jnp.stack(sides, axis=1)


def shards(density, basis_in, basis_out, points, nodes, near_rows, send_leaf, adm_slot):
    leaves, fields, leaf_size = density.shape
    rank_size = basis_in.shape[1]
    deep_count = lax.axis_size("deep")
    devices = lax.axis_size("wide") * deep_count
    capacity = send_leaf.shape[2]
    axes = ("wide", "deep")
    send = send_leaf.reshape(devices * capacity)
    deep_points = passed_along(points, "deep", -1)
    wide_points = passed_along(points, "wide", -1)
    outgoing = outgoing_blocks(send, basis_in, density)
    outgoing = outgoing.reshape(devices, capacity * outgoing.shape[1], outgoing.shape[2])
    block_rows = outgoing.shape[1]
    padded = jnp.pad(nodes, ((0, 0), (0, 1), (0, 0))).reshape(leaves, -1)[send]
    out_nodes = padded.reshape(devices, -1, outgoing.shape[2])
    outgoing = jnp.concatenate([outgoing, out_nodes], axis=1)
    arrived = lax.all_to_all(outgoing, axes, split_axis=0, concat_axis=0, tiled=True)
    table = arrived[:, :block_rows].reshape(devices * capacity, rank_size // 2, 2 * fields)
    table_nodes = arrived[:, block_rows:].reshape(devices * capacity, 4, rank_size)[:, :3]
    far_nodes = as_targets(table_nodes)
    far_nodes = halves_repeated(far_nodes)

    my_device = lax.axis_index("wide") * deep_count + lax.axis_index("deep")
    point_table = as_targets(jnp.concatenate([points, deep_points, wide_points], axis=0))
    offset = near_rows // leaves - my_device
    region = jnp.where(offset == 0, 0, jnp.where(offset == 1, 1, 2))
    codes = region * leaves + near_rows % leaves
    own, for_deep, for_wide = near_sums(codes, as_sources(points), point_table, density)
    from_deep = passed_along(for_deep, "deep", 1)
    from_wide = passed_along(for_wide, "wide", 1)
    far_field = far_sums(adm_slot, as_sources(nodes), far_nodes, table, basis_out)
    return far_field + (own + from_deep.astype(jnp.float32) + from_wide.astype(jnp.float32))


def solution(mesh):
    split = ("wide", "deep")
    in_specs = (
        P(split, None, None),
        P(split, None, None),
        P(split, None, None),
        P(split, None, None),
        P(split, None, None),
        P(split, None),
        P(split, None, None),
        P(split, None),
    )
    return jax.shard_map(
        shards, mesh=mesh, in_specs=in_specs, out_specs=P(split, None, None), check_vma=False
    )
```
